32 devices in a mesh: rep: 2 (over y), seq: 4 (over z), head: 2 (over x), sub: 2 (over core).
Axes of the slice: x: 2, y: 2, z: 4, core: 2. Of those that a mesh axis runs over, the one named last changes fastest.
Arguments:
- key_cache: float32 [8, 32768, 128], P('head', ('rep', 'seq')), parts along dimension 1, may hold values from -40 to 40
- value_cache: bfloat16 [8, 32768, 128], P('head', ('rep', 'seq')), parts along dimension 1, may hold values from -6 to 6
- centroids: float32 [8, 1024, 128], P('head', ('rep', 'sub')), parts along dimension 1, may hold values from -8 to 8
- inv_temp: float32 [8], P('head'), may hold values from 0.015625 to 0.078125
- page_owner: int32 [8, 256, 1], P('head', ('rep', 'seq')), parts along dimension 1, may hold values from 0 to 3; in each aligned block of 32 rows (0 to 31, 32 to 63, ..., all dimensions but the last counted through in order) at most 12 rows name the same one
Outputs:
- clusters: float32 [8, 1024, 128], P('head', ('rep', 'sub')), parts along dimension 1
- moved_keys: bfloat16 [8, 384, 128, 128], P('head', ('rep', 'seq')), parts along dimension 1
- moved_values: bfloat16 [8, 384, 128, 128], P('head', ('rep', 'seq')), parts along dimension 1
- page_ids: int32 [8, 384], P('head', ('rep', 'seq')), parts along dimension 1
The draws below stay inside these ranges and needn't reach their ends.
There are 2 independent parts, one for each index of `rep`. The reference program is written for one: setup_inputs(seed, part) draws one part's arguments, and reference() takes and returns one part's arrays. A program takes and returns all parts, laid end to end along the dimension named above; an argument that names none is the same for every part. Nothing has to cross between parts.
Inputs may be any that keep to these rules, and one draw needn't show every extreme that they name: `page_owner`: among the 32 pages of one head on one index of seq (an aligned block), no owner is named by more than 12 pages, a bound that some block reaches.
All inputs are finite; a program needn't handle non-finite values.
Results may differ from the reference program's by a relative error of at most 0.0075.
Values may be sent and summed in bfloat16 or wider, within the bound.
A program may use at most 128 MiB of HBM per device.

```python
import math
import jax
import jax.numpy as jnp
import numpy as np
from jax import lax

HEADS = 8
DH = 128
CENT = 512
ITERS = 3
PAGE = 128
TOKENS = 16384
PAGE_DEV = 32
PAGES = 128
CAP = 12
SLOTS = 192
N_SEQ = 4


def cluster_centers(key):
    base_draw = jax.random.normal(jax.random.fold_in(key, 11), (HEADS, CENT, DH), jnp.float32)
    return 0.6 * base_draw + 0.8 * jnp.roll(base_draw, 1, axis=1)


def draw_key_cache(key, part):
    centers = cluster_centers(key)
    positions = jnp.arange(TOKENS, dtype=jnp.int32)
    jitter = jax.random.randint(jax.random.fold_in(key, 12), (HEADS, TOKENS), 0, 4)
    labels = (positions[None, :] * CENT // TOKENS + jitter) % CENT
    located = jax.vmap(lambda table_rows, label_rows: jnp.take(table_rows, label_rows, axis=0))(centers, labels)
    noise = 0.5 * jax.random.normal(jax.random.fold_in(key, 13), (HEADS, TOKENS, DH), jnp.float32)
    marked = (positions % 509 == 0)[None, :, None]
    amplitude = (30 + 5 * (positions // 509 % 3)).astype(jnp.float32)[None, :, None]
    loud = amplitude * jnp.sign(located)
    drawn = jnp.where(marked, loud, located + noise)
    return jnp.clip(drawn, -40.0, 40.0)


def draw_centroids(key, part):
    centers = cluster_centers(key)
    noise = jax.random.normal(jax.random.fold_in(key, 15), (HEADS, CENT, DH), jnp.float32)
    drawn = centers + 0.3 * noise
    return jnp.clip(drawn, -8.0, 8.0)


def steps_of(stream_key, dims, shards, low, top_value):
    level, own = 1.0, jax.random.fold_in(stream_key, 6)
    for axis_at, parts in shards:
        draws = jnp.exp(jax.random.uniform(jax.random.fold_in(own, axis_at), (parts,), jnp.float32, low / len(shards), top_value / len(shards)))
        level = level * jnp.repeat(draws, dims[axis_at] // parts).reshape([-1 if axis == axis_at else 1 for axis in range(len(dims))])
    return level


def routed_block(stream_key, own, number, rows, count, top, reach, lean):
    sequence = jax.random.permutation(stream_key, count)
    crowded, usual = portions_of(count, rows * top, reach, lean, True), portions_of(count, rows * top, reach, lean, False)
    places = jnp.arange(count)

    def named(tallies, rotation):
        used = int((tallies > 0).sum())
        fixed = max(1, used // 4)
        passed = fixed + (places - fixed + rotation * (used - fixed)) % max(1, count - fixed)
        return jnp.zeros((count,), jnp.int32).at[sequence[jnp.where(places < fixed, places, passed)]].set(jnp.asarray(tallies, jnp.int32))

    tallies = jnp.where(number % 4 == 0, named(crowded, number // 4), named(usual, number - number // 4 - 1))
    mixed = jax.random.permutation(jax.random.fold_in(own, 3), count)
    donor, sink = mixed[0:count // 2 * 2:2], mixed[1:count // 2 * 2:2]
    margin = jnp.minimum(tallies[donor] - 1, reach - tallies[sink]) // 2
    margin = jnp.where((donor == sequence[0]) | (sink == sequence[0]) | (tallies[sink] == 0), 0, jnp.maximum(margin, 0))
    passed = jax.random.randint(jax.random.fold_in(own, 4), (count // 2,), 0, 1 << 20) % (margin + 1)
    tallies = tallies.at[donor].add(-passed).at[sink].add(passed)
    members = jnp.searchsorted(jnp.cumsum(tallies), jnp.arange(rows * top), side="right").astype(jnp.int32)
    listing = members.reshape(top, rows).T
    listing = listing[jax.random.permutation(jax.random.fold_in(own, 1), rows)]
    rotation = jax.random.randint(jax.random.fold_in(own, 2), (rows, 1), 0, top)
    return jnp.take_along_axis(listing, (jnp.arange(top)[None, :] + rotation) % top, axis=1)


def portions_of(count, total, limit, lean, full):
    portions = [(1 << 20) // math.isqrt(standing ** lean) + 1 for standing in range(1, count + 1)]
    largest = limit if full else min(limit, max(-(-total // count), total * portions[0] // sum(portions)))
    least = 1 if total - largest >= count - 1 else 0
    holding, rest = [largest] + [least] * (count - 1), total - largest - least * (count - 1)
    while rest > 0:
        candidates = [i for i in range(1, count) if holding[i] < largest] or [i for i in range(1, count) if holding[i] < limit]
        pool, remaining = sum([portions[i] for i in candidates]), rest
        for i in candidates:
            more = min(limit - holding[i], max(1, remaining * portions[i] // pool), rest)
            holding[i] = holding[i] + more
            rest = rest - more
    return np.array(holding)


def normal_values(own_key, extent, deviation, limit, shards=(), kind=jnp.bfloat16):
    result = deviation * jax.random.normal(own_key, extent, jnp.float32)
    if shards:
        result = result * steps_of(own_key, extent, shards, -0.22, 0.18)
    return jnp.clip(result, -limit, limit).astype(kind)


def setup_inputs(seed: int = 0, part: int = 0) -> dict:
    seeds = jax.random.split(jax.random.key(seed), 6)
    part_keys = jax.random.split(jax.random.fold_in(seeds[5], part), 6)
    key_cache = draw_key_cache(jax.random.fold_in(jax.random.fold_in(seeds[5], part), 71), part)
    value_cache = normal_values(part_keys[1], (HEADS, TOKENS, DH), 1.0, 6.0, ((0, 2), (1, 4)))
    centroids = draw_centroids(jax.random.fold_in(jax.random.fold_in(seeds[5], part), 71), part)
    inv_temp = jnp.clip(jnp.exp(math.log(0.078125) - 1.609438 * jax.random.uniform(seeds[3], (HEADS,), jnp.float32) ** steps_of(seeds[3], (HEADS,), ((0, 2),), -0.2, 0.2)), 0.015625, 0.078125)
    page_owner_keys = jax.random.split(jax.random.fold_in(part_keys[4], 1), HEADS * PAGES // PAGE_DEV)
    page_owner_turns = jax.random.permutation(jax.random.fold_in(part_keys[4], 3), HEADS * PAGES // PAGE_DEV)
    page_owner = jax.vmap(lambda own, number: routed_block(jax.random.fold_in(part_keys[4], 2), own, number, PAGE_DEV, N_SEQ, 1, CAP, 2))(page_owner_keys, page_owner_turns).reshape((HEADS, PAGES, 1))
    return {"key_cache": key_cache, "value_cache": value_cache, "centroids": centroids, "inv_temp": inv_temp, "page_owner": page_owner}


prior_count = 8.0


def page_slots(page_owner, owner_count, capacity):
    owner_ids = jnp.arange(owner_count, dtype=jnp.int32)
    owner_hits = (page_owner[:, None, :] == owner_ids[None, :, None]).astype(jnp.int32)
    before = jnp.cumsum(owner_hits, axis=2) - owner_hits
    slot_ids = jnp.arange(capacity, dtype=jnp.int32)
    matched = (owner_hits[:, :, None, :] == 1) & (before[:, :, None, :] == slot_ids[None, None, :, None])
    page_index = jnp.arange(page_owner.shape[1], dtype=jnp.int32)
    source = jnp.sum(jnp.where(matched, page_index[None, None, None, :], 0), axis=3).astype(jnp.int32)
    filled = jnp.any(matched, axis=3)
    head_count = page_owner.shape[0]
    return source.reshape(head_count, owner_count * capacity), filled.reshape(head_count, owner_count * capacity)


def head_sweep(operands):
    keys_head, cent_head, head_rate = operands
    low_table = cent_head.astype(jnp.bfloat16)
    half_norm = 0.5 * jnp.sum(cent_head * cent_head, axis=1)
    scores = jnp.dot(keys_head, low_table.T, preferred_element_type=jnp.float32)
    logits = head_rate * (scores - half_norm[None, :])
    highest = jnp.max(logits, axis=1, keepdims=True)
    spread = jnp.exp(logits - highest)
    weights = (spread / jnp.sum(spread, axis=1, keepdims=True)).astype(jnp.bfloat16)
    key_sums = jnp.dot(weights.T, keys_head, preferred_element_type=jnp.float32)
    resp_mass = jnp.sum(weights.astype(jnp.float32), axis=0)
    return (key_sums + prior_count * cent_head) / (resp_mass[:, None] + prior_count)


def pick_pages(page_rows, global_index, filled):
    picked = jax.vmap(lambda head_block, row_index: jnp.take(head_block, row_index, axis=0))(page_rows, global_index)
    return jnp.where(filled[:, :, None, None], picked, jnp.zeros((), page_rows.dtype))


def reference(key_cache, value_cache, centroids, inv_temp, page_owner):
    keys_low = key_cache.astype(jnp.bfloat16)
    cent_table = centroids
    for iteration in range(ITERS):
        cent_table = lax.map(head_sweep, (keys_low, cent_table, inv_temp))
    clusters = cent_table

    owner_grid = page_owner[:, :, 0].reshape(HEADS, N_SEQ, PAGE_DEV)
    source, filled = jax.vmap(lambda owner_rows: page_slots(owner_rows, N_SEQ, CAP), in_axes=1, out_axes=1)(owner_grid)
    source = source.reshape(HEADS, N_SEQ, N_SEQ, CAP)
    filled = filled.reshape(HEADS, N_SEQ, N_SEQ, CAP)
    source_base = (PAGE_DEV * jnp.arange(N_SEQ, dtype=jnp.int32))[None, :, None, None]
    global_index = (source + source_base).astype(jnp.int32)
    global_index = jnp.transpose(global_index, (0, 2, 1, 3)).reshape(HEADS, SLOTS)
    filled = jnp.transpose(filled, (0, 2, 1, 3)).reshape(HEADS, SLOTS)
    page_ids = jnp.where(filled, global_index, -1).astype(jnp.int32)
    moved_keys = pick_pages(keys_low.reshape(HEADS, PAGES, PAGE, DH), global_index, filled)
    moved_values = pick_pages(value_cache.reshape(HEADS, PAGES, PAGE, DH), global_index, filled)
    return (clusters, moved_keys, moved_values, page_ids)
```

```python
import functools
import math

import jax
import jax.numpy as jnp
from jax import lax
from jax.experimental import pallas as pl
from jax.experimental.pallas import tpu as pltpu
from jax.sharding import PartitionSpec as P

ITERS = 3
PAGE = 128
LANES = 128
TILE = 512
MESH = pl.DeviceIdType.MESH

prior_count = 8.0


def page_slots(page_owner, owner_count, capacity):
    pages = page_owner.shape[1]
    index = jnp.arange(pages, dtype=jnp.int32)
    same = page_owner[:, :, None] == page_owner[:, None, :]
    rank = jnp.sum(jnp.where(same & (index[None, :] < index[:, None]), 1, 0), axis=2)
    place = page_owner * capacity + rank
    slot_ids = jnp.arange(owner_count * capacity, dtype=jnp.int32)
    hits = place[:, None, :] == slot_ids[None, :, None]
    return jnp.sum(jnp.where(hits, index + 1, 0), axis=2) - 1


def gather_kernel(share, owners, capacity, slots_ref, first_ref, key_ref, value_ref,
                  low_ref, send_key_ref, send_value_ref):
    base = (first_ref[0] + pl.program_id(0)) * (owners * capacity)
    low_ref[0] = key_ref[0].astype(jnp.bfloat16)
    for owner in range(owners):
        for slot in range(capacity):
            page = slots_ref[base + owner * capacity + slot]
            filled = page >= 0
            page = jnp.maximum(page, 0)
            rows = pl.ds(pl.multiple_of(page * PAGE, PAGE), PAGE)

            @pl.when(filled)
            def _():
                send_key_ref[owner, 0, slot] = key_ref[0, rows, :].astype(jnp.bfloat16)
                send_value_ref[owner, 0, slot] = value_ref[0, rows, :]

            @pl.when(jnp.logical_not(filled))
            def _():
                send_key_ref[owner, 0, slot] = jnp.zeros((PAGE, LANES), jnp.bfloat16)
                send_value_ref[owner, 0, slot] = jnp.zeros((PAGE, LANES), jnp.bfloat16)


def partner(me, step, owners):
    out = 0
    bit = 1
    while bit < owners:
        own = lax.rem(lax.div(me, bit), 2)
        out = out + lax.rem(own + (1 if step & bit else 0), 2) * bit
        bit *= 2
    return out


def cluster_kernel(owners, share, capacity, low_ref, cent_ref, rate_ref, ids_ref,
                   send_key_ref, send_value_ref,
                   clusters_ref, moved_key_ref, moved_value_ref, moved_ids_ref,
                   keys_aug, table, table_aug, acc, part, part_in, mass, mass_in, total_rep,
                   ids_in, fin,
                   page_sems, fwd_sems, own_sems, own_fwd_sems, sum_sems, mass_sems, table_sems,
                   ids_sems, cent_sems, fin_sems):
    me = lax.axis_index("seq")
    sub = lax.axis_index("sub")
    sib = 1 - sub
    cents = table.shape[2]
    half = cent_ref.shape[1]
    quarter = cents // owners
    tokens = low_ref.shape[1]
    partners = [partner(me, step, owners) for step in range(1, owners)]

    barrier = pltpu.get_barrier_semaphore()
    for q in partners:
        pl.semaphore_signal(barrier, inc=1, device_id={"seq": q}, device_id_type=MESH)
    pl.semaphore_signal(barrier, inc=1, device_id={"sub": sib}, device_id_type=MESH)
    pl.semaphore_wait(barrier, owners)

    def remote(src, dst, sems, at, device):
        return pltpu.make_async_remote_copy(
            src_ref=src, dst_ref=dst, send_sem=sems.at[(0, *at)], recv_sem=sems.at[(1, *at)],
            device_id=device, device_id_type=MESH,
        )

    waits = []
    first_head = sub * share
    cent_copy = remote(cent_ref.at[pl.ds(sib * share, share)],
                       table.at[0, :, pl.ds(pl.multiple_of(sub * half, half), half), :],
                       cent_sems, (), {"sub": sib})
    cent_copy.start()
    ids_copies = []
    for i, q in enumerate(partners):
        c = remote(ids_ref.at[q], ids_in.at[me], ids_sems, (i,), {"seq": q})
        c.start()
        ids_copies.append(c)

    arrays = ((send_key_ref, moved_key_ref), (send_value_ref, moved_value_ref))
    my_slots = pl.ds(me * capacity, capacity)
    own_copies = []
    for a, (src, dst) in enumerate(arrays):
        for h in range(share):
            c = pltpu.make_async_copy(src.at[me, h], dst.at[first_head + h, my_slots],
                                      own_sems.at[a, h])
            c.start()
            f = remote(src.at[me, h], dst.at[first_head + h, my_slots], own_fwd_sems, (a, h),
                       {"sub": sib})
            f.start()
            own_copies += [(c, f)]
    order = []
    far = [i for i in range(owners - 1) if i + 1 >= owners // 2]
    near = [i for i in range(owners - 1) if i + 1 < owners // 2]
    far_list = [(i, a, h) for i in reversed(far) for a in range(2) for h in range(share)]
    near_list = [(i, a, h) for i in reversed(near) for a in range(2) for h in range(share)]
    while far_list or near_list:
        take = 2 if near_list else len(far_list)
        order += far_list[:take]
        far_list = far_list[take:]
        order += near_list[:1]
        near_list = near_list[1:]
    page_copies = []
    for i, a, h in order:
        src, dst = arrays[a]
        q = partners[i]
        page_copies.append((
            remote(src.at[q, h], dst.at[first_head + h, my_slots], page_sems, (i, a, h), {"seq": q}),
            remote(dst.at[first_head + h, pl.ds(q * capacity, capacity)],
                   dst.at[first_head + h, pl.ds(q * capacity, capacity)],
                   fwd_sems, (i, a, h), {"sub": sib}),
        ))
    phases = 2 * ITERS
    started = [0]

    def start_pages(upto):
        while started[0] < min(upto, len(page_copies)):
            page_copies[started[0]][0].start()
            started[0] += 1

    step_pages = max(1, len(page_copies) // (2 * phases))
    start_pages(2 * step_pages)

    for h in range(share):
        keys_aug[h, :, :LANES] = low_ref[h]
        keys_aug[h, :, LANES:] = jnp.ones((tokens, LANES), jnp.bfloat16)
        table[0, h, pl.ds(pl.multiple_of(sub * half, half), half), :] = cent_ref[first_head + h]
    cent_copy.wait()

    lane = lax.broadcasted_iota(jnp.int32, (cents, LANES), 1)
    eye = (lax.broadcasted_iota(jnp.int32, (LANES, LANES), 0)
           == lax.broadcasted_iota(jnp.int32, (LANES, LANES), 1))
    blocks = cents // LANES
    for it in range(ITERS):
        for h in range(share):
            rows = table[it, h]
            norm = jnp.broadcast_to(-0.5 * jnp.sum(rows * rows, axis=1, keepdims=True), rows.shape)
            high = norm.astype(jnp.bfloat16).astype(jnp.float32)
            rest = norm - high
            mid = rest.astype(jnp.bfloat16).astype(jnp.float32)
            low = rest - mid
            extra = jnp.where(lane == 0, high, jnp.where(lane == 1, mid, jnp.where(lane == 2, low, 0.0)))
            table_aug[h, :, :LANES] = rows.astype(jnp.bfloat16)
            table_aug[h, :, LANES:] = extra.astype(jnp.bfloat16)
            acc[h] = jnp.zeros((cents, 2 * LANES), jnp.float32)
            rate = rate_ref[h, 0:1, 0:1] * (1.0 / math.log(2.0))

            def sweep(i, carry, h=h, rate=rate):
                k = keys_aug[h, pl.ds(pl.multiple_of(i * TILE, TILE), TILE), :]
                s = lax.dot_general(table_aug[h], k, (((1,), (1,)), ((), ())),
                                    preferred_element_type=jnp.float32)
                top = jnp.max(s, axis=0, keepdims=True)
                p = jnp.exp2((s - top) * rate)
                w = (p * (1.0 / jnp.sum(p, axis=0, keepdims=True))).astype(jnp.bfloat16)
                acc[h] += jnp.dot(w, k, preferred_element_type=jnp.float32)
                return carry

            lax.fori_loop(0, tokens // TILE, sweep, 0)
        for h in range(share):
            part[it, h] = acc[h, :, :LANES].astype(jnp.bfloat16)
            for b in range(blocks):
                rep = acc[h, b * LANES:(b + 1) * LANES, LANES:]
                mass[it, h * blocks + b:h * blocks + b + 1, :] = jnp.sum(
                    jnp.where(eye, rep, 0.0), axis=0, keepdims=True)
        copies = []
        for i, q in enumerate(partners):
            c = remote(part.at[it, :, pl.ds(pl.multiple_of(q * quarter, quarter), quarter), :],
                       part_in.at[it, i], sum_sems, (it, i), {"seq": q})
            m = remote(mass.at[it], mass_in.at[it, i], mass_sems, (it, i), {"seq": q})
            c.start()
            m.start()
            copies += [c, m]
        start_pages((3 + 2 * it) * step_pages)
        for c in copies:
            c.wait()
        masses = mass[it]
        for i in range(owners - 1):
            masses = masses + mass_in[it, i]
        mine = pl.ds(pl.multiple_of(me * quarter, quarter), quarter)
        for h in range(share):
            for b in range(blocks):
                row = masses[h * blocks + b:h * blocks + b + 1, :]
                total_rep[b * LANES:(b + 1) * LANES, :] = jnp.broadcast_to(
                    jnp.sum(jnp.where(eye, row, 0.0), axis=1, keepdims=True), (LANES, LANES))
            sums = acc[h, mine, :LANES]
            for i in range(owners - 1):
                sums = sums + part_in[it, i, h].astype(jnp.float32)
            table[it + 1, h, mine, :] = (sums + prior_count * table[it, h, mine, :]) / (
                total_rep[mine, :] + prior_count)
        copies = []
        for i, q in enumerate(partners):
            c = remote(table.at[it + 1, :, mine, :], table.at[it + 1, :, mine, :],
                       table_sems, (it, i), {"seq": q})
            c.start()
            copies.append(c)
        start_pages((4 + 2 * it) * step_pages)
        for c in copies:
            c.wait()

    start_pages(len(page_copies))
    fin_copy = remote(table.at[ITERS, :, pl.ds(pl.multiple_of(sib * half, half), half), :], fin,
                      fin_sems, (), {"sub": sib})
    fin_copy.start()
    for h in range(share):
        clusters_ref[first_head + h] = table[ITERS, h, pl.ds(pl.multiple_of(sub * half, half), half), :]
    fin_copy.wait()
    for h in range(share):
        clusters_ref[sib * share + h] = fin[h]
    for c in ids_copies:
        c.wait()
    ids_in[me] = ids_ref[me]
    moved_ids_ref[...] = ids_in[...]
    for c, f in own_copies:
        c.wait()
        f.wait()
    for c, f in page_copies:
        c.wait_recv()
        f.start()
    for c, f in page_copies:
        c.wait_send()
        f.wait()


def on_device(key_cache, value_cache, centroids, inv_temp, page_owner):
    heads, tokens, width = key_cache.shape
    pages = tokens // PAGE
    owners = lax.axis_size("seq")
    capacity = max(2, (3 * pages + 2 * owners - 1) // (2 * owners))
    share = heads // lax.axis_size("sub")
    half = centroids.shape[1]
    cents = half * lax.axis_size("sub")
    quarter = cents // owners
    first = lax.axis_index("sub") * share
    slots = page_slots(page_owner[:, :, 0], owners, capacity)
    ids = jnp.where(slots >= 0, slots + lax.axis_index("seq") * pages, -1)
    ids = jnp.transpose(ids.reshape(heads, owners, capacity), (1, 0, 2))
    ids = jnp.pad(ids, ((0, 0), (0, 8 - heads), (0, LANES - capacity)))

    low = jax.ShapeDtypeStruct((share, tokens, width), jnp.bfloat16)
    sent = jax.ShapeDtypeStruct((owners, share, capacity, PAGE, width), jnp.bfloat16)
    keys_low, send_keys, send_values = pl.pallas_call(
        functools.partial(gather_kernel, share, owners, capacity),
        out_shape=(low, sent, sent),
        grid_spec=pltpu.PrefetchScalarGridSpec(
            num_scalar_prefetch=2,
            grid=(share,),
            in_specs=[
                pl.BlockSpec((1, tokens, width), lambda h, s, f: (f[0] + h, 0, 0)),
                pl.BlockSpec((1, tokens, width), lambda h, s, f: (f[0] + h, 0, 0)),
            ],
            out_specs=[
                pl.BlockSpec((1, tokens, width), lambda h, s, f: (h, 0, 0)),
                pl.BlockSpec((owners, 1, capacity, PAGE, width), lambda h, s, f: (0, h, 0, 0, 0)),
                pl.BlockSpec((owners, 1, capacity, PAGE, width), lambda h, s, f: (0, h, 0, 0, 0)),
            ],
        ),
        compiler_params=pltpu.CompilerParams(vmem_limit_bytes=40 * 2**20),
        name="gather_pages",
    )(slots.reshape(-1), first.reshape(1), key_cache, value_cache)

    rates = jnp.broadcast_to(
        lax.dynamic_slice_in_dim(inv_temp, first, share, 0)[:, None, None], (share, 8, LANES))
    moved = jax.ShapeDtypeStruct((heads, owners * capacity, PAGE, width), jnp.bfloat16)
    vmem = pl.BlockSpec(memory_space=pltpu.VMEM)
    anyspace = pl.BlockSpec(memory_space=pl.ANY)
    dma = pltpu.SemaphoreType.DMA
    rest = owners - 1
    clusters, moved_keys, moved_values, moved_ids = pl.pallas_call(
        functools.partial(cluster_kernel, owners, share, capacity),
        out_shape=(
            jax.ShapeDtypeStruct(centroids.shape, jnp.float32), moved, moved,
            jax.ShapeDtypeStruct((owners, 8, LANES), jnp.int32),
        ),
        in_specs=[vmem, vmem, vmem, vmem, anyspace, anyspace],
        out_specs=[vmem, anyspace, anyspace, vmem],
        scratch_shapes=[
            pltpu.VMEM((share, tokens, 2 * LANES), jnp.bfloat16),
            pltpu.VMEM((ITERS + 1, share, cents, width), jnp.float32),
            pltpu.VMEM((share, cents, 2 * LANES), jnp.bfloat16),
            pltpu.VMEM((share, cents, 2 * LANES), jnp.float32),
            pltpu.VMEM((ITERS, share, cents, width), jnp.bfloat16),
            pltpu.VMEM((ITERS, rest, share, quarter, width), jnp.bfloat16),
            pltpu.VMEM((ITERS, 8, LANES), jnp.float32),
            pltpu.VMEM((ITERS, rest, 8, LANES), jnp.float32),
            pltpu.VMEM((cents, LANES), jnp.float32),
            pltpu.VMEM((owners, 8, LANES), jnp.int32),
            pltpu.VMEM((share, half, width), jnp.float32),
            dma((2, rest, 2, share)),
            dma((2, rest, 2, share)),
            dma((2, share)),
            dma((2, 2, share)),
            dma((2, ITERS, rest)),
            dma((2, ITERS, rest)),
            dma((2, ITERS, rest)),
            dma((2, rest)),
            dma((2,)),
            dma((2,)),
        ],
        compiler_params=pltpu.CompilerParams(
            collective_id=0, has_side_effects=True, vmem_limit_bytes=48 * 2**20),
        name="cluster_and_move",
    )(keys_low, centroids, rates, ids, send_keys, send_values)
    moved_ids = jnp.transpose(moved_ids[:, :heads, :capacity], (1, 0, 2)).reshape(heads, owners * capacity)
    return clusters, moved_keys, moved_values, moved_ids


def solution(mesh):
    return jax.shard_map(
        on_device,
        mesh=mesh,
        in_specs=(
            P("head", ("rep", "seq"), None),
            P("head", ("rep", "seq"), None),
            P("head", ("rep", "sub"), None),
            P("head"),
            P("head", ("rep", "seq"), None),
        ),
        out_specs=(
            P("head", ("rep", "sub"), None),
            P("head", ("rep", "seq"), None, None),
            P("head", ("rep", "seq"), None, None),
            P("head", ("rep", "seq")),
        ),
        check_vma=False,
    )
```

```python
import functools
import math

import jax
import jax.numpy as jnp
from jax import lax
from jax.experimental import pallas as pl
from jax.experimental.pallas import tpu as pltpu
from jax.sharding import PartitionSpec as P

ITERS = 3
PAGE = 128
LANES = 128
TILE = 512
MESH = pl.DeviceIdType.MESH

prior_count = 8.0


def page_slots(page_owner, owner_count, capacity):
    pages = page_owner.shape[1]
    index = jnp.arange(pages, dtype=jnp.int32)
    same = page_owner[:, :, None] == page_owner[:, None, :]
    rank = jnp.sum(jnp.where(same & (index[None, :] < index[:, None]), 1, 0), axis=2)
    place = page_owner * capacity + rank
    slot_ids = jnp.arange(owner_count * capacity, dtype=jnp.int32)
    hits = place[:, None, :] == slot_ids[None, :, None]
    return jnp.sum(jnp.where(hits, index + 1, 0), axis=2) - 1


def gather_kernel(share, owners, capacity, slots_ref, first_ref, key_ref, value_ref,
                  low_ref, send_key_ref, send_value_ref):
    base = (first_ref[0] + pl.program_id(0)) * (owners * capacity)
    low_ref[0] = key_ref[0].astype(jnp.bfloat16)
    for owner in range(owners):
        for slot in range(capacity):
            page = slots_ref[base + owner * capacity + slot]
            filled = page >= 0
            page = jnp.maximum(page, 0)
            rows = pl.ds(pl.multiple_of(page * PAGE, PAGE), PAGE)

            @pl.when(filled)
            def _():
                send_key_ref[owner, 0, slot] = key_ref[0, rows, :].astype(jnp.bfloat16)
                send_value_ref[owner, 0, slot] = value_ref[0, rows, :]

            @pl.when(jnp.logical_not(filled))
            def _():
                send_key_ref[owner, 0, slot] = jnp.zeros((PAGE, LANES), jnp.bfloat16)
                send_value_ref[owner, 0, slot] = jnp.zeros((PAGE, LANES), jnp.bfloat16)


def partner(me, step, owners):
    out = 0
    bit = 1
    while bit < owners:
        own = lax.rem(lax.div(me, bit), 2)
        out = out + lax.rem(own + (1 if step & bit else 0), 2) * bit
        bit *= 2
    return out


def cluster_kernel(owners, share, capacity, low_ref, cent_ref, rate_ref, ids_ref,
                   send_key_ref, send_value_ref,
                   clusters_ref, moved_key_ref, moved_value_ref, moved_ids_ref,
                   keys_aug, keys_across, table, table_aug, acc, part, part_in, mass, mass_in, total_rep,
                   norm_rep, norm, norm_in, low_table, ids_in, fin,
                   page_sems, fwd_sems, own_sems, own_fwd_sems, sum_sems, mass_sems, table_sems, norm_sems,
                   ids_sems, cent_sems, fin_sems):
    me = lax.axis_index("seq")
    sub = lax.axis_index("sub")
    sib = 1 - sub
    cents = table.shape[1]
    half = cent_ref.shape[1]
    quarter = cents // owners
    tokens = low_ref.shape[1]
    partners = [partner(me, step, owners) for step in range(1, owners)]

    barrier = pltpu.get_barrier_semaphore()
    for q in partners:
        pl.semaphore_signal(barrier, inc=1, device_id={"seq": q}, device_id_type=MESH)
    pl.semaphore_signal(barrier, inc=1, device_id={"sub": sib}, device_id_type=MESH)
    pl.semaphore_wait(barrier, owners)

    def remote(src, dst, sems, at, device):
        return pltpu.make_async_remote_copy(
            src_ref=src, dst_ref=dst, send_sem=sems.at[(0, *at)], recv_sem=sems.at[(1, *at)],
            device_id=device, device_id_type=MESH,
        )

    waits = []
    first_head = sub * share
    cent_copy = remote(cent_ref.at[pl.ds(sib * share, share)],
                       table.at[:, pl.ds(pl.multiple_of(sub * half, half), half), :],
                       cent_sems, (), {"sub": sib})
    cent_copy.start()
    ids_copies = []
    for i, q in enumerate(partners):
        c = remote(ids_ref.at[q], ids_in.at[me], ids_sems, (i,), {"seq": q})
        c.start()
        ids_copies.append(c)

    arrays = ((send_key_ref, moved_key_ref), (send_value_ref, moved_value_ref))
    my_slots = pl.ds(me * capacity, capacity)
    own_copies = []
    for a, (src, dst) in enumerate(arrays):
        for h in range(share):
            c = pltpu.make_async_copy(src.at[me, h], dst.at[first_head + h, my_slots],
                                      own_sems.at[a, h])
            c.start()
            f = remote(src.at[me, h], dst.at[first_head + h, my_slots], own_fwd_sems, (a, h),
                       {"sub": sib})
            f.start()
            own_copies += [(c, f)]
    order = []
    far = [i for i in range(owners - 1) if i + 1 >= owners // 2]
    near = [i for i in range(owners - 1) if i + 1 < owners // 2]
    far_list = [(i, a, h) for i in reversed(far) for a in range(2) for h in range(share)]
    near_list = [(i, a, h) for i in reversed(near) for a in range(2) for h in range(share)]
    while far_list or near_list:
        take = 2 if near_list else len(far_list)
        order += far_list[:take]
        far_list = far_list[take:]
        order += near_list[:1]
        near_list = near_list[1:]
    page_copies = []
    for i, a, h in order:
        src, dst = arrays[a]
        q = partners[i]
        page_copies.append((
            remote(src.at[q, h], dst.at[first_head + h, my_slots], page_sems, (i, a, h), {"seq": q}),
            remote(dst.at[first_head + h, pl.ds(q * capacity, capacity)],
                   dst.at[first_head + h, pl.ds(q * capacity, capacity)],
                   fwd_sems, (i, a, h), {"sub": sib}),
        ))
    phases = 2 * ITERS
    started = [0]

    def start_pages(upto):
        while started[0] < min(upto, len(page_copies)):
            page_copies[started[0]][0].start()
            started[0] += 1

    step_pages = max(1, len(page_copies) // (2 * phases))
    start_pages(2 * step_pages)

    for h in range(share):
        keys_aug[h, :, :LANES] = low_ref[h]
        keys_aug[h, :, LANES:] = jnp.ones((tokens, LANES), jnp.bfloat16)
        keys_across[h, LANES:, :] = jnp.ones((LANES, tokens), jnp.bfloat16)

        def turn(i, carry, h=h):
            cols = pl.ds(pl.multiple_of(i * TILE, TILE), TILE)
            keys_across[h, :LANES, cols] = jnp.swapaxes(low_ref[h, cols, :], 0, 1)
            return carry

        lax.fori_loop(0, tokens // TILE, turn, 0)
        table[h, pl.ds(pl.multiple_of(sub * half, half), half), :] = cent_ref[first_head + h]
    norm_rep[...] = jnp.zeros(norm_rep.shape, jnp.float32)
    norm[...] = jnp.zeros(norm.shape, jnp.float32)
    mass[...] = jnp.zeros(mass.shape, jnp.float32)
    cent_copy.wait()

    lane = lax.broadcasted_iota(jnp.int32, (cents, LANES), 1)
    eye = (lax.broadcasted_iota(jnp.int32, (LANES, LANES), 0)
           == lax.broadcasted_iota(jnp.int32, (LANES, LANES), 1))
    blocks = cents // LANES
    for it in range(ITERS):
        for h in range(share):
            if it == 0:
                rows = table[h]
                half_norm = jnp.broadcast_to(-0.5 * jnp.sum(rows * rows, axis=1, keepdims=True), rows.shape)
                table_aug[h, :, :LANES] = rows.astype(jnp.bfloat16)
            else:
                for b in range(blocks):
                    row = norms[h * blocks + b:h * blocks + b + 1, :]
                    total_rep[b * LANES:(b + 1) * LANES, :] = jnp.broadcast_to(
                        jnp.sum(jnp.where(eye, row, 0.0), axis=1, keepdims=True), (LANES, LANES))
                half_norm = total_rep[...]
                table_aug[h, :, :LANES] = low_table[it - 1, h]
            high = half_norm.astype(jnp.bfloat16).astype(jnp.float32)
            rest = half_norm - high
            mid = rest.astype(jnp.bfloat16).astype(jnp.float32)
            low = rest - mid
            extra = jnp.where(lane == 0, high, jnp.where(lane == 1, mid, jnp.where(lane == 2, low, 0.0)))
            table_aug[h, :, LANES:] = extra.astype(jnp.bfloat16)
            acc[h] = jnp.zeros((cents, 2 * LANES), jnp.float32)
        rates = [rate_ref[h, 0:1, 0:1] * (1.0 / math.log(2.0)) for h in range(share)]

        def sweep(i, carry, rates=rates):
            cols = pl.ds(pl.multiple_of(i * TILE, TILE), TILE)
            scores = [jnp.dot(table_aug[h], keys_across[h, :, cols],
                              preferred_element_type=jnp.float32) for h in range(share)]
            for h, s in enumerate(scores):
                top = jnp.max(s, axis=0, keepdims=True)
                p = jnp.exp2((s - top) * rates[h])
                w = (p * (1.0 / jnp.sum(p, axis=0, keepdims=True))).astype(jnp.bfloat16)
                acc[h] += jnp.dot(w, keys_aug[h, cols, :], preferred_element_type=jnp.float32)
            return carry

        lax.fori_loop(0, tokens // TILE, sweep, 0)
        for h in range(share):
            part[it, h] = acc[h, :, :LANES].astype(jnp.bfloat16)
            for b in range(blocks):
                rep = acc[h, b * LANES:(b + 1) * LANES, LANES:]
                mass[it, h * blocks + b:h * blocks + b + 1, :] = jnp.sum(
                    jnp.where(eye, rep, 0.0), axis=0, keepdims=True)
        copies = []
        for i, q in enumerate(partners):
            c = remote(part.at[it, :, pl.ds(pl.multiple_of(q * quarter, quarter), quarter), :],
                       part_in.at[it, i], sum_sems, (it, i), {"seq": q})
            m = remote(mass.at[it], mass_in.at[it, i], mass_sems, (it, i), {"seq": q})
            c.start()
            m.start()
            copies += [c, m]
        start_pages((3 + 2 * it) * step_pages)
        for c in copies:
            c.wait()
        masses = mass[it]
        for i in range(owners - 1):
            masses = masses + mass_in[it, i]
        mine = pl.ds(pl.multiple_of(me * quarter, quarter), quarter)
        for h in range(share):
            for b in range(blocks):
                row = masses[h * blocks + b:h * blocks + b + 1, :]
                total_rep[b * LANES:(b + 1) * LANES, :] = jnp.broadcast_to(
                    jnp.sum(jnp.where(eye, row, 0.0), axis=1, keepdims=True), (LANES, LANES))
            sums = acc[h, mine, :LANES]
            for i in range(owners - 1):
                sums = sums + part_in[it, i, h].astype(jnp.float32)
            fresh = (sums + prior_count * table[h, mine, :]) / (total_rep[mine, :] + prior_count)
            table[h, mine, :] = fresh
            low_table[it, h, mine, :] = fresh.astype(jnp.bfloat16)
            if it + 1 < ITERS:
                norm_rep[mine, :] = jnp.broadcast_to(
                    -0.5 * jnp.sum(fresh * fresh, axis=1, keepdims=True), fresh.shape)
                for b in range(blocks):
                    norm[it, h * blocks + b:h * blocks + b + 1, :] = jnp.sum(
                        jnp.where(eye, norm_rep[b * LANES:(b + 1) * LANES, :], 0.0), axis=0, keepdims=True)
        copies = []
        for i, q in enumerate(partners):
            c = remote(low_table.at[it, :, mine, :], low_table.at[it, :, mine, :],
                       table_sems, (it, i), {"seq": q})
            c.start()
            copies.append(c)
            if it + 1 < ITERS:
                m = remote(norm.at[it], norm_in.at[it, i], norm_sems, (it, i), {"seq": q})
                m.start()
                copies.append(m)
        start_pages((4 + 2 * it) * step_pages)
        for c in copies:
            c.wait()
        if it + 1 < ITERS:
            norms = norm[it]
            for i in range(owners - 1):
                norms = norms + norm_in[it, i]

    start_pages(len(page_copies))
    fin_copy = remote(low_table.at[ITERS - 1, :, pl.ds(pl.multiple_of(sib * half, half), half), :], fin,
                      fin_sems, (), {"sub": sib})
    fin_copy.start()
    for h in range(share):
        clusters_ref[first_head + h] = low_table[
            ITERS - 1, h, pl.ds(pl.multiple_of(sub * half, half), half), :].astype(jnp.float32)
    fin_copy.wait()
    for h in range(share):
        clusters_ref[sib * share + h] = fin[h].astype(jnp.float32)
    for c in ids_copies:
        c.wait()
    ids_in[me] = ids_ref[me]
    moved_ids_ref[...] = ids_in[...]
    for c, f in own_copies:
        c.wait()
        f.wait()
    for c, f in page_copies:
        c.wait_recv()
        f.start()
    for c, f in page_copies:
        c.wait_send()
        f.wait()


def on_device(key_cache, value_cache, centroids, inv_temp, page_owner):
    heads, tokens, width = key_cache.shape
    pages = tokens // PAGE
    owners = lax.axis_size("seq")
    capacity = max(2, (3 * pages + 2 * owners - 1) // (2 * owners))
    share = heads // lax.axis_size("sub")
    half = centroids.shape[1]
    cents = half * lax.axis_size("sub")
    quarter = cents // owners
    first = lax.axis_index("sub") * share
    slots = page_slots(page_owner[:, :, 0], owners, capacity)
    ids = jnp.where(slots >= 0, slots + lax.axis_index("seq") * pages, -1)
    ids = jnp.transpose(ids.reshape(heads, owners, capacity), (1, 0, 2))
    ids = jnp.pad(ids, ((0, 0), (0, 8 - heads), (0, LANES - capacity)))

    low = jax.ShapeDtypeStruct((share, tokens, width), jnp.bfloat16)
    sent = jax.ShapeDtypeStruct((owners, share, capacity, PAGE, width), jnp.bfloat16)
    keys_low, send_keys, send_values = pl.pallas_call(
        functools.partial(gather_kernel, share, owners, capacity),
        out_shape=(low, sent, sent),
        grid_spec=pltpu.PrefetchScalarGridSpec(
            num_scalar_prefetch=2,
            grid=(share,),
            in_specs=[
                pl.BlockSpec((1, tokens, width), lambda h, s, f: (f[0] + h, 0, 0)),
                pl.BlockSpec((1, tokens, width), lambda h, s, f: (f[0] + h, 0, 0)),
            ],
            out_specs=[
                pl.BlockSpec((1, tokens, width), lambda h, s, f: (h, 0, 0)),
                pl.BlockSpec((owners, 1, capacity, PAGE, width), lambda h, s, f: (0, h, 0, 0, 0)),
                pl.BlockSpec((owners, 1, capacity, PAGE, width), lambda h, s, f: (0, h, 0, 0, 0)),
            ],
        ),
        compiler_params=pltpu.CompilerParams(vmem_limit_bytes=40 * 2**20),
        name="gather_pages",
    )(slots.reshape(-1), first.reshape(1), key_cache, value_cache)

    rates = jnp.broadcast_to(
        lax.dynamic_slice_in_dim(inv_temp, first, share, 0)[:, None, None], (share, 8, LANES))
    moved = jax.ShapeDtypeStruct((heads, owners * capacity, PAGE, width), jnp.bfloat16)
    vmem = pl.BlockSpec(memory_space=pltpu.VMEM)
    anyspace = pl.BlockSpec(memory_space=pl.ANY)
    dma = pltpu.SemaphoreType.DMA
    rest = owners - 1
    clusters, moved_keys, moved_values, moved_ids = pl.pallas_call(
        functools.partial(cluster_kernel, owners, share, capacity),
        out_shape=(
            jax.ShapeDtypeStruct(centroids.shape, jnp.float32), moved, moved,
            jax.ShapeDtypeStruct((owners, 8, LANES), jnp.int32),
        ),
        in_specs=[vmem, vmem, vmem, vmem, anyspace, anyspace],
        out_specs=[vmem, anyspace, anyspace, vmem],
        scratch_shapes=[
            pltpu.VMEM((share, tokens, 2 * LANES), jnp.bfloat16),
            pltpu.VMEM((share, 2 * LANES, tokens), jnp.bfloat16),
            pltpu.VMEM((share, cents, width), jnp.float32),
            pltpu.VMEM((share, cents, 2 * LANES), jnp.bfloat16),
            pltpu.VMEM((share, cents, 2 * LANES), jnp.float32),
            pltpu.VMEM((ITERS, share, cents, width), jnp.bfloat16),
            pltpu.VMEM((ITERS, rest, share, quarter, width), jnp.bfloat16),
            pltpu.VMEM((ITERS, 8, LANES), jnp.float32),
            pltpu.VMEM((ITERS, rest, 8, LANES), jnp.float32),
            pltpu.VMEM((cents, LANES), jnp.float32),
            pltpu.VMEM((cents, LANES), jnp.float32),
            pltpu.VMEM((ITERS, 8, LANES), jnp.float32),
            pltpu.VMEM((ITERS, rest, 8, LANES), jnp.float32),
            pltpu.VMEM((ITERS, share, cents, width), jnp.bfloat16),
            pltpu.VMEM((owners, 8, LANES), jnp.int32),
            pltpu.VMEM((share, half, width), jnp.bfloat16),
            dma((2, rest, 2, share)),
            dma((2, rest, 2, share)),
            dma((2, share)),
            dma((2, 2, share)),
            dma((2, ITERS, rest)),
            dma((2, ITERS, rest)),
            dma((2, ITERS, rest)),
            dma((2, ITERS, rest)),
            dma((2, rest)),
            dma((2,)),
            dma((2,)),
        ],
        compiler_params=pltpu.CompilerParams(
            collective_id=0, has_side_effects=True, vmem_limit_bytes=40 * 2**20),
        name="cluster_and_move",
    )(keys_low, centroids, rates, ids, send_keys, send_values)
    moved_ids = jnp.transpose(moved_ids[:, :heads, :capacity], (1, 0, 2)).reshape(heads, owners * capacity)
    return clusters, moved_keys, moved_values, moved_ids


def solution(mesh):
    return jax.shard_map(
        on_device,
        mesh=mesh,
        in_specs=(
            P("head", ("rep", "seq"), None),
            P("head", ("rep", "seq"), None),
            P("head", ("rep", "sub"), None),
            P("head"),
            P("head", ("rep", "seq"), None),
        ),
        out_specs=(
            P("head", ("rep", "sub"), None),
            P("head", ("rep", "seq"), None, None),
            P("head", ("rep", "seq"), None, None),
            P("head", ("rep", "seq")),
        ),
        check_vma=False,
    )
```
